32 devices in a mesh: grp: 2 (over x), tile: 2 (over core), cond: 8 (over z, y).
Axes of the slice: x: 2, y: 2, z: 4, core: 2. Of those that a mesh axis runs over, the one named last changes fastest.
Arguments:
- latent: float32 [4096, 128], P(('grp', 'cond'), 'tile'), parts along dimension 0, may hold values from -8 to 8
- target: int32 [4096, 128], P('grp'), parts along dimension 0, may hold values 0 or 1
- kernel_table: float32 [8, 8, 2, 65, 65], replicated, may hold values from -4.5 to 4.5
- socs_weights: float32 [8], replicated, may hold values from 0.25 to 2.5
- dose_levels: float32 [4], replicated, may hold values from 0.8 to 1.25
- cond_focus: int32 [8], replicated, may hold values from 0 to 7, each once
- cond_dose: int32 [8], replicated, may hold values from 0 to 3
Outputs:
- mask_gradient: float32 [4096, 128], P(('grp', 'cond'), 'tile'), parts along dimension 0
- worst_loss: float32 [2], P('grp'), parts along dimension 0
The draws below stay inside these ranges and needn't reach their ends.
There are 2 independent parts, one for each index of `grp`. The reference program is written for one: setup_inputs(seed, part) draws one part's arguments, and reference() takes and returns one part's arrays. A program takes and returns all parts, laid end to end along the dimension named above; an argument that names none is the same for every part. Nothing has to cross between parts.
Inputs may be any that keep to these rules, and one draw needn't show every extreme that they name: `cond_focus`: each focus level is named by exactly one condition.
All inputs are finite; a program needn't handle non-finite values.
Results may differ from the reference program's by a relative error of at most 0.0003.
Values sent between devices are 32-bit elements; how exact they have to be, the bound alone decides.
A program may use at most 64 MiB of HBM per device.

```python
import math
import jax
import jax.numpy as jnp
from jax import lax

TILE = 128
HALO = 16
NF = 65
KERNELS = 8
NDOSE = 4
EXT = 160
NROWS = 2048
CONDS = 8
NFOCUS = 8
NPIX = 262144


def set_ends(array, stream_key, smallest, high):
    longest = array.shape.index(max(array.shape))
    spots = []
    for shift in (0, 1):
        where = [jax.random.randint(jax.random.fold_in(stream_key, axis), (), 0, length) for axis, length in enumerate(array.shape)]
        where[longest] = (where[longest] + shift) % array.shape[longest]
        spots.append(tuple(where))
    return array.at[spots[0]].set(smallest).at[spots[1]].set(high)


def levels(stream_key, shape, pieces, smallest, largest):
    factor_of, own = 1.0, jax.random.fold_in(stream_key, 6)
    for dim, parts in pieces:
        draws = jnp.exp(jax.random.uniform(jax.random.fold_in(own, dim), (parts,), jnp.float32, smallest / len(pieces), largest / len(pieces)))
        factor_of = factor_of * jnp.repeat(draws, shape[dim] // parts).reshape([-1 if axis == dim else 1 for axis in range(len(shape))])
    return factor_of


def gaussian(rng, dims, width, bound, cuts=(), kind=jnp.bfloat16):
    values = jax.random.normal(rng, dims, jnp.float32) * width
    if len(cuts) > 0:
        values = levels(rng, dims, cuts, -0.22, 0.18) * values
    return jnp.clip(values, min=-bound, max=bound).astype(kind)


def setup_inputs(seed: int = 0, part: int = 0) -> dict:
    keys = jax.random.split(jax.random.key(seed), 8)
    own_keys = jax.random.split(jax.random.fold_in(keys[7], part), 8)
    return {
        "latent": gaussian(own_keys[0], (NROWS, TILE), 2.0, 8.0, ((0, 8), (1, 2)), jnp.float32),
        "target": set_ends((jax.random.randint(own_keys[1], (NROWS, TILE), 0, 5) < 2).astype(jnp.int32), jax.random.fold_in(own_keys[1], 1), 0, 1),
        "kernel_table": gaussian(keys[2], (NFOCUS, KERNELS, 2, NF, NF), 0.75, 4.5, (), jnp.float32),
        "socs_weights": jnp.clip(jnp.exp(jax.random.uniform(keys[3], (KERNELS,), jnp.float32, math.log(0.25), math.log(2.5))), 0.25, 2.5),
        "dose_levels": jnp.clip(jnp.exp(jax.random.uniform(keys[4], (NDOSE,), jnp.float32, math.log(0.8), math.log(1.25))), 0.8, 1.25),
        "cond_focus": jax.random.permutation(keys[5], CONDS).astype(jnp.int32),
        "cond_dose": set_ends(jax.random.randint(keys[6], (CONDS,), 0, NDOSE), jax.random.fold_in(keys[6], 1), 0, NDOSE - 1).astype(jnp.int32),
    }


STEEPNESS = 4.0
THRESHOLD = 1.0
SHARPNESS = 6.0
GRAD_GAIN = 256.0
PRECISE = lax.Precision.HIGHEST

def make_tables(freq_count, period, offset, extent):
    frequency = jnp.arange(freq_count, dtype=jnp.int32) - (freq_count - 1) // 2
    position = jnp.arange(extent, dtype=jnp.int32) + offset
    product = frequency[:, None] * position[None, :] % period
    phases = product.astype(jnp.float32) * (2.0 * math.pi / period)
    return (jnp.cos(phases), jnp.sin(phases))

def tile_error(tile_block, spectra, weights, dose, target_tile, tables):
    cos_full, sin_full, cos_core, sin_core = tables
    col_real = jnp.dot(tile_block, cos_core.T, precision=PRECISE)
    col_imag = -jnp.dot(tile_block, sin_core.T, precision=PRECISE)
    spec_real = jnp.dot(cos_full, col_real, precision=PRECISE) + jnp.dot(sin_full, col_imag, precision=PRECISE)
    spec_imag = jnp.dot(cos_full, col_imag, precision=PRECISE) - jnp.dot(sin_full, col_real, precision=PRECISE)
    inverse_area = 1.0 / (cos_full.shape[1] * cos_full.shape[1])
    kern_real = spectra[:, 0]
    kern_imag = spectra[:, 1]
    prod_real = (kern_real * spec_real - kern_imag * spec_imag) * inverse_area
    prod_imag = (kern_real * spec_imag + kern_imag * spec_real) * inverse_area
    half_real = jnp.einsum('kfg,gy->kfy', prod_real, cos_core, precision=PRECISE) - jnp.einsum('kfg,gy->kfy', prod_imag, sin_core, precision=PRECISE)
    half_imag = jnp.einsum('kfg,gy->kfy', prod_real, sin_core, precision=PRECISE) + jnp.einsum('kfg,gy->kfy', prod_imag, cos_core, precision=PRECISE)
    field_real = jnp.einsum('fx,kfy->kxy', cos_core, half_real, precision=PRECISE) - jnp.einsum('fx,kfy->kxy', sin_core, half_imag, precision=PRECISE)
    field_imag = jnp.einsum('fx,kfy->kxy', cos_core, half_imag, precision=PRECISE) + jnp.einsum('fx,kfy->kxy', sin_core, half_real, precision=PRECISE)
    intensity = lax.optimization_barrier(jnp.sum(weights[:, None, None] * (field_real * field_real + field_imag * field_imag), axis=0))
    resist = jax.nn.sigmoid(STEEPNESS * (dose * intensity - THRESHOLD))
    missed = resist - target_tile
    return jnp.sum(missed * missed)

def reference(latent, target, kernel_table, socs_weights, dose_levels, cond_focus, cond_dose):
    mask = jax.nn.sigmoid(latent)
    padded = jnp.pad(mask, ((HALO, HALO), (0, 0)))
    cos_full, sin_full = make_tables(NF, EXT, 0, EXT)
    cos_core, sin_core = make_tables(NF, EXT, HALO, TILE)
    tables = (cos_full, sin_full, cos_core, sin_core)
    tile_count = NROWS // TILE
    targets = target.astype(jnp.float32).reshape(tile_count, TILE, TILE)
    spectra_all = kernel_table[cond_focus]
    dose_values = dose_levels[cond_dose]
    tile_ids = jnp.arange(tile_count, dtype=jnp.int32)
    anchor = jnp.int32(0)

    def cond_error(packed):
        spectra, dose = packed

        def one_tile(index):
            tile_block = lax.dynamic_slice(padded, ((index * TILE).astype(jnp.int32), anchor), (EXT, TILE))
            target_tile = lax.dynamic_index_in_dim(targets, index, 0, keepdims=False)
            return tile_error(tile_block, spectra, socs_weights, dose, target_tile, tables)
        return jnp.sum(lax.map(one_tile, tile_ids))
    errors = lax.map(cond_error, (spectra_all, dose_values))
    scores = SHARPNESS * errors / NPIX
    exponent = jnp.exp(scores)
    denominator = jnp.sum(exponent)
    worst_loss = (jnp.log(denominator) / SHARPNESS).reshape(1)
    cond_weights = exponent / denominator

    def advance(gradient, index):
        row_start = (index * TILE).astype(jnp.int32)
        tile_block = lax.dynamic_slice(padded, (row_start, anchor), (EXT, TILE))
        target_tile = lax.dynamic_index_in_dim(targets, index, 0, keepdims=False)

        def cond_grad(packed):
            spectra, dose, weight = packed
            _, pullback = jax.vjp(lambda blocked: tile_error(blocked, spectra, socs_weights, dose, target_tile, tables), tile_block)
            return pullback(weight)[0]
        increment = lax.optimization_barrier(jnp.sum(lax.map(cond_grad, (spectra_all, dose_values, cond_weights)), axis=0))
        current = lax.dynamic_slice(gradient, (row_start, anchor), (EXT, TILE))
        return (lax.dynamic_update_slice(gradient, current + increment, (row_start, anchor)), None)
    gradient, _ = lax.scan(advance, jnp.zeros(padded.shape, jnp.float32), tile_ids)
    central = gradient[HALO:HALO + NROWS]
    mask_gradient = GRAD_GAIN * central * (mask * (1.0 - mask))
    return (mask_gradient, worst_loss)
```

```python
import functools
import math

import jax
import jax.numpy as jnp
import ml_dtypes
import numpy as np
from jax import lax
from jax.experimental import pallas as pl
from jax.experimental.pallas import tpu as pltpu
from jax.sharding import PartitionSpec as P

TILE = 128
HALO = 16
NF = 65
EXT = 160
FP = 80
GP = 128

STEEPNESS = 4.0
THRESHOLD = 1.0
SHARPNESS = 6.0
GRAD_GAIN = 256.0
MESH = pl.DeviceIdType.MESH
BF = jnp.bfloat16


def halves(table):
    high = table.astype(np.float32).astype(ml_dtypes.bfloat16)
    low = (table - high.astype(np.float64)).astype(np.float32).astype(ml_dtypes.bfloat16)
    return high, low


def left_table(table):
    high, low = halves(table)
    return np.concatenate([high, high, low], axis=1)


def right_table(table):
    high, low = halves(table)
    return np.concatenate([high, high, low], axis=0)


def make_tables(parts):
    freq = np.arange(NF) - (NF - 1) // 2

    def waves(positions, rows):
        phase = 2.0 * math.pi * ((freq[:, None] * positions[None, :]) % EXT) / EXT
        pad = ((0, rows - NF), (0, 0))
        return np.pad(np.cos(phase), pad), np.pad(np.sin(phase), pad)

    core = np.arange(TILE) + HALO
    cos_full, sin_full = waves(np.arange(EXT), FP)
    cos_rows, sin_rows = waves(core, FP)
    cos_lane, sin_lane = waves(core, GP)
    width = TILE // parts
    cols = np.concatenate([cos_lane.T, -sin_lane.T], axis=1)
    col_halves = [cols[h * width : (h + 1) * width] for h in range(parts)]
    col_high = np.stack([halves(c)[0] for c in col_halves])
    col_low = np.stack([halves(c)[1] for c in col_halves])
    col_back = np.stack([right_table(c.T) for c in col_halves])
    spec = np.block([[cos_full, sin_full], [-sin_full, cos_full]])
    rows = np.block([[cos_rows.T, -sin_rows.T], [sin_rows.T, cos_rows.T]])
    field = np.block([[cos_lane, sin_lane], [-sin_lane, cos_lane]])
    return (
        col_high,
        col_low,
        col_back,
        left_table(spec),
        left_table(spec.T),
        left_table(rows),
        left_table(rows.T),
        right_table(field),
        right_table(field.T),
    )


def split(values):
    high = values.astype(BF)
    low = (values - high.astype(jnp.float32)).astype(BF)
    return high, low


def mul(a, b):
    return jnp.dot(a, b, preferred_element_type=jnp.float32)


def data_left(values, table):
    high, low = split(values)
    return mul(jnp.concatenate([high, low, high], axis=1), table)


def data_right(table, values):
    high, low = split(values)
    return mul(table, jnp.concatenate([high, low, high], axis=0))


def kernel(
    sizes,
    latent_ref,
    target_hbm,
    table_hbm,
    socs_ref,
    dose_ref,
    focus_ref,
    level_ref,
    col_high,
    col_low,
    col_back,
    spec_tab,
    spec_back,
    row_tab,
    row_back,
    field_tab,
    field_back,
    grad_out,
    loss_out,
    mask,
    raw,
    kern,
    target,
    spec,
    field,
    slope,
    dspec,
    grad,
    peer_grad,
    upper,
    lower,
    errors,
    local_sem,
    mask_send,
    mask_recv,
    err_send,
    err_recv,
    grad_send,
    grad_recv,
):
    parts, groups, rows, conds, kernels, pixels, all_conds, doses = sizes
    g = lax.axis_index("grp")
    j = lax.axis_index("tile")
    i = lax.axis_index("cond")
    tiles = rows // TILE
    me = i * parts + j
    everyone = parts * groups
    inverse_area = 1.0 / (EXT * EXT)

    table_copy = pltpu.make_async_copy(
        table_hbm.at[pl.ds(j * conds, conds)], raw, local_sem.at[0]
    )
    table_copy.start()
    target_copy = pltpu.make_async_copy(
        target_hbm.at[pl.ds(i * rows, rows)], target, local_sem.at[1]
    )
    target_copy.start()

    errors[j, i] = jnp.zeros(errors.shape[2:], jnp.float32)
    upper[...] = jnp.zeros_like(upper)
    lower[...] = jnp.zeros_like(lower)

    barrier = pltpu.get_barrier_semaphore()

    def greet(step, carry):
        other = (me + step) % everyone
        pl.semaphore_signal(
            barrier, inc=1, device_id=(g, other % parts, other // parts), device_id_type=MESH
        )
        return carry

    lax.fori_loop(1, everyone, greet, 0)

    mask_own = jax.nn.sigmoid(latent_ref[...])
    mask[j, HALO : HALO + rows, :] = mask_own
    grad[...] = jnp.zeros_like(grad)

    @pl.when(i == 0)
    def _():
        for h in range(parts):
            mask[h, 0:HALO, :] = jnp.zeros((HALO, TILE // parts), jnp.float32)

    @pl.when(i == groups - 1)
    def _():
        for h in range(parts):
            mask[h, HALO + rows :, :] = jnp.zeros((HALO, TILE // parts), jnp.float32)

    pl.semaphore_wait(barrier, everyone - 1)

    def mask_peer(d):
        block = mask.at[j, pl.ds(HALO, rows)]
        return pltpu.make_async_remote_copy(
            block, block, mask_send.at[d], mask_recv.at[d],
            device_id=(g, (j + d) % parts, i), device_id_type=MESH,
        )

    def mask_edge(up, d):
        src = mask.at[j, pl.ds(HALO, HALO)] if up else mask.at[j, pl.ds(rows, HALO)]
        dst = mask.at[j, pl.ds(HALO + rows, HALO)] if up else mask.at[j, pl.ds(0, HALO)]
        slot = parts + (0 if up else parts) + d
        return pltpu.make_async_remote_copy(
            src, dst, mask_send.at[slot], mask_recv.at[slot],
            device_id=(g, (j + d) % parts, i - 1 if up else i + 1), device_id_type=MESH,
        )

    for d in range(1, parts):
        mask_peer(d).start()

    @pl.when(i > 0)
    def _():
        for d in range(parts):
            mask_edge(True, d).start()

    @pl.when(i < groups - 1)
    def _():
        for d in range(parts):
            mask_edge(False, d).start()

    table_copy.wait()
    kern[...] = jnp.zeros_like(kern)

    def pad_kernels(c, carry):
        for k in range(kernels):
            for part in range(2):
                kern[c, k, part, 0:NF, 0:NF] = raw[c, k, part]
        return carry

    lax.fori_loop(0, conds, pad_kernels, 0)

    target_copy.wait()

    for d in range(1, parts):
        mask_peer(d).wait()

    @pl.when(i > 0)
    def _():
        for d in range(parts):
            mask_edge(True, d).wait_send()
            mask_edge(False, d).wait_recv()

    @pl.when(i < groups - 1)
    def _():
        for d in range(parts):
            mask_edge(False, d).wait_send()
            mask_edge(True, d).wait_recv()

    for t in range(tiles):
        cols = None
        for h in range(parts):
            high, low = split(mask[h, t * TILE : t * TILE + EXT, :])
            term = mul(high, col_high[h]) + mul(low, col_high[h]) + mul(high, col_low[h])
            cols = term if cols is None else cols + term
        stacked = jnp.concatenate([cols[:, :GP], cols[:, GP:]], axis=0)
        spec[t] = data_right(spec_tab[...], stacked) * inverse_area

    cond_doses = []
    for c in range(all_conds):
        value = jnp.float32(0.0)
        for n in range(doses):
            value = jnp.where(level_ref[c] == n, dose_ref[n], value)
        cond_doses.append(value)

    def forward(index, carry):
        c = index // tiles
        t = index % tiles
        dose = jnp.float32(0.0)
        for n in range(all_conds):
            dose = jnp.where(focus_ref[n] == j * conds + c, cond_doses[n], dose)
        spec_real = spec[t, 0:FP, :]
        spec_imag = spec[t, FP:, :]
        columns = []
        for k in range(kernels):
            kern_real = kern[c, k, 0]
            kern_imag = kern[c, k, 1]
            prod = jnp.concatenate(
                [
                    kern_real * spec_real - kern_imag * spec_imag,
                    kern_real * spec_imag + kern_imag * spec_real,
                ],
                axis=0,
            )
            high, low = split(prod)
            columns.append(jnp.concatenate([high, low, high], axis=0))
        half = mul(row_tab[...], jnp.concatenate(columns, axis=1))
        left = []
        for k in range(kernels):
            part = half[:, k * GP : (k + 1) * GP]
            high, low = split(jnp.concatenate([part[:TILE], part[TILE:]], axis=1))
            left.append(jnp.concatenate([high, low, high], axis=1))
        image = mul(jnp.concatenate(left, axis=0), field_tab[...])
        field[index] = image
        intensity = jnp.zeros((TILE, TILE), jnp.float32)
        for k in range(kernels):
            part = image[k * TILE : (k + 1) * TILE]
            real, imag = part[:, :TILE], part[:, TILE:]
            intensity = intensity + socs_ref[k] * (real * real + imag * imag)
        resist = jax.nn.sigmoid(STEEPNESS * (dose * intensity - THRESHOLD))
        wanted = target[pl.ds(pl.multiple_of(t * TILE, TILE), TILE), :].astype(jnp.float32)
        missed = resist - wanted
        slope[index] = (4.0 * STEEPNESS) * dose * (missed * (resist * (1.0 - resist)))
        sums = jnp.sum(missed * missed, axis=0, keepdims=True)
        errors[j, i, pl.ds(c, 1), :] = errors[j, i, pl.ds(c, 1), :] + sums
        return carry

    lax.fori_loop(0, conds * tiles, forward, 0)

    def err_copy(step):
        other = (me + step) % everyone
        block = errors.at[j, i]
        return pltpu.make_async_remote_copy(
            block, block, err_send.at[step], err_recv.at[step],
            device_id=(g, other % parts, other // parts), device_id_type=MESH,
        )

    def send_error(step, carry):
        err_copy(step).start()
        return carry

    lax.fori_loop(1, everyone, send_error, 0)

    def backward(index, carry):
        c = index // tiles
        t = index % tiles
        gain = slope[index]
        left = []
        for k in range(kernels):
            part = field[index, k * TILE : (k + 1) * TILE, :]
            scale = socs_ref[k] * gain
            high, low = split(
                jnp.concatenate([part[:, :TILE] * scale, part[:, TILE:] * scale], axis=1)
            )
            left.append(jnp.concatenate([high, low, high], axis=1))
        half = mul(jnp.concatenate(left, axis=0), field_back[...])
        columns = []
        for k in range(kernels):
            part = half[k * TILE : (k + 1) * TILE]
            high, low = split(jnp.concatenate([part[:, :GP], part[:, GP:]], axis=0))
            columns.append(jnp.concatenate([high, low, high], axis=0))
        prod = mul(row_back[...], jnp.concatenate(columns, axis=1))
        real = jnp.zeros((FP, GP), jnp.float32)
        imag = jnp.zeros((FP, GP), jnp.float32)
        for k in range(kernels):
            prod_real = prod[:FP, k * GP : (k + 1) * GP]
            prod_imag = prod[FP:, k * GP : (k + 1) * GP]
            kern_real = kern[c, k, 0]
            kern_imag = kern[c, k, 1]
            real = real + (kern_real * prod_real + kern_imag * prod_imag)
            imag = imag + (kern_real * prod_imag - kern_imag * prod_real)
        dspec[index, 0:FP, :] = real
        dspec[index, FP:, :] = imag
        return carry

    lax.fori_loop(0, conds * tiles, backward, 0)

    def wait_error(step, carry):
        err_copy(step).wait()
        return carry

    lax.fori_loop(1, everyone, wait_error, 0)

    slots = errors.shape[2]
    valid = lax.broadcasted_iota(jnp.int32, (slots, 1), 0) < conds
    denominator = jnp.zeros((1, 1), jnp.float32)
    mine = jnp.zeros((slots, 1), jnp.float32)
    for h in range(parts):
        total = errors[h, 0]
        for n in range(1, groups):
            total = total + errors[h, n]
        score = SHARPNESS * jnp.sum(total, axis=1, keepdims=True) / pixels
        exponent = jnp.where(valid, jnp.exp(score), 0.0)
        denominator = denominator + jnp.sum(exponent, axis=0, keepdims=True)
        mine = jnp.where(j == h, exponent, mine)
    weights = mine / denominator
    loss_out[...] = jnp.broadcast_to(jnp.log(denominator) / SHARPNESS, loss_out.shape)

    for t in range(tiles):
        total = jnp.zeros((2 * FP, GP), jnp.float32)
        for c in range(conds):
            total = total + weights[c : c + 1, :] * dspec[c * tiles + t]
        stacked = data_right(spec_back[...], total * inverse_area)
        wide = jnp.concatenate([stacked[:EXT], stacked[EXT:]], axis=1)
        high, low = split(wide)
        left = jnp.concatenate([high, low, high], axis=1)
        for h in range(parts):
            window = (h, slice(t * TILE, t * TILE + EXT), slice(None))
            grad[window] = grad[window] + mul(left, col_back[h])

    def grad_peer(d):
        return pltpu.make_async_remote_copy(
            grad.at[(j + d) % parts, pl.ds(HALO, rows)], peer_grad.at[d - 1],
            grad_send.at[d], grad_recv.at[d],
            device_id=(g, (j + d) % parts, i), device_id_type=MESH,
        )

    def grad_edge(up, d):
        to = (j + d) % parts
        src = grad.at[to, pl.ds(0, HALO)] if up else grad.at[to, pl.ds(HALO + rows, HALO)]
        dst = lower.at[d] if up else upper.at[d]
        slot = parts + (0 if up else parts) + d
        return pltpu.make_async_remote_copy(
            src, dst, grad_send.at[slot], grad_recv.at[slot],
            device_id=(g, to, i - 1 if up else i + 1), device_id_type=MESH,
        )

    @pl.when(i > 0)
    def _():
        for d in range(parts):
            grad_edge(True, d).start()

    @pl.when(i < groups - 1)
    def _():
        for d in range(parts):
            grad_edge(False, d).start()

    for d in range(1, parts):
        grad_peer(d).start()

    own = mask[j, HALO : HALO + rows, :]
    scale = GRAD_GAIN * (own * (1.0 - own))
    total = grad[j, HALO : HALO + rows, :]

    for d in range(1, parts):
        grad_peer(d).wait()
        total = total + peer_grad[d - 1]

    @pl.when(i > 0)
    def _():
        for d in range(parts):
            grad_edge(True, d).wait_send()
            grad_edge(False, d).wait_recv()

    @pl.when(i < groups - 1)
    def _():
        for d in range(parts):
            grad_edge(False, d).wait_send()
            grad_edge(True, d).wait_recv()

    head, tail = upper[0], lower[0]
    for d in range(1, parts):
        head = head + upper[d]
        tail = tail + lower[d]
    grad_out[...] = total * scale
    grad_out[0:HALO, :] = (total[0:HALO] + head) * scale[0:HALO]
    grad_out[rows - HALO :, :] = (total[rows - HALO :] + tail) * scale[rows - HALO :]


def shards(latent, target, kernel_table, socs_weights, dose_levels, cond_focus, cond_dose):
    parts = lax.axis_size("tile")
    groups = lax.axis_size("cond")
    rows, width = latent.shape
    kernels = kernel_table.shape[1]
    all_conds = cond_focus.shape[0]
    conds = all_conds // parts
    tiles = rows // TILE
    pixels = rows * groups * TILE
    tables = [jnp.asarray(table) for table in make_tables(parts)]
    sizes = (parts, groups, rows, conds, kernels, pixels, all_conds, dose_levels.shape[0])
    slots = -(-conds // 8) * 8
    vmem = pl.BlockSpec(memory_space=pltpu.VMEM)
    smem = pl.BlockSpec(memory_space=pltpu.SMEM)
    anywhere = pl.BlockSpec(memory_space=pl.ANY)
    f32 = jnp.float32
    everyone = parts * groups
    mask_gradient, loss = pl.pallas_call(
        functools.partial(kernel, sizes),
        out_shape=(
            jax.ShapeDtypeStruct((rows, width), f32),
            jax.ShapeDtypeStruct((8, 128), f32),
        ),
        in_specs=[vmem, anywhere, anywhere, smem, smem, smem, smem] + [vmem] * len(tables),
        out_specs=(vmem, vmem),
        scratch_shapes=[
            pltpu.VMEM((parts, rows + 2 * HALO, width), f32),
            pltpu.VMEM((conds,) + kernel_table.shape[1:], f32),
            pltpu.VMEM((conds, kernels, 2, FP, GP), f32),
            pltpu.VMEM((rows, TILE), jnp.int32),
            pltpu.VMEM((tiles, 2 * FP, GP), f32),
            pltpu.VMEM((conds * tiles, kernels * TILE, 2 * TILE), f32),
            pltpu.VMEM((conds * tiles, TILE, TILE), f32),
            pltpu.VMEM((conds * tiles, 2 * FP, GP), f32),
            pltpu.VMEM((parts, rows + 2 * HALO, width), f32),
            pltpu.VMEM((max(parts - 1, 1), rows, width), f32),
            pltpu.VMEM((parts, HALO, width), f32),
            pltpu.VMEM((parts, HALO, width), f32),
            pltpu.VMEM((parts, groups, slots, TILE), f32),
            pltpu.SemaphoreType.DMA((2,)),
            pltpu.SemaphoreType.DMA((3 * parts,)),
            pltpu.SemaphoreType.DMA((3 * parts,)),
            pltpu.SemaphoreType.DMA((everyone,)),
            pltpu.SemaphoreType.DMA((everyone,)),
            pltpu.SemaphoreType.DMA((3 * parts,)),
            pltpu.SemaphoreType.DMA((3 * parts,)),
        ],
        compiler_params=pltpu.CompilerParams(
            collective_id=0, has_side_effects=True, vmem_limit_bytes=56 * 1024 * 1024
        ),
        name="litho",
    )(
        latent, target, kernel_table, socs_weights, dose_levels, cond_focus, cond_dose, *tables
    )
    return (mask_gradient, loss[0, :1])


def solution(mesh):
    in_specs = (P(("grp", "cond"), "tile"), P("grp", None), P(), P(), P(), P(), P())
    out_specs = (P(("grp", "cond"), "tile"), P("grp"))
    return jax.shard_map(shards, mesh=mesh, in_specs=in_specs, out_specs=out_specs, check_vma=False)
```

```python
import functools
import math

import jax
import jax.numpy as jnp
import ml_dtypes
import numpy as np
from jax import lax
from jax.experimental import pallas as pl
from jax.experimental.pallas import tpu as pltpu
from jax.sharding import PartitionSpec as P

TILE = 128
HALO = 16
NF = 65
EXT = 160
FP = 80
GP = 128

STEEPNESS = 4.0
THRESHOLD = 1.0
SHARPNESS = 6.0
GRAD_GAIN = 256.0
MESH = pl.DeviceIdType.MESH
BF = jnp.bfloat16


def halves(table):
    high = table.astype(np.float32).astype(ml_dtypes.bfloat16)
    low = (table - high.astype(np.float64)).astype(np.float32).astype(ml_dtypes.bfloat16)
    return high, low


def left_table(table):
    high, low = halves(table)
    return np.concatenate([high, high, low], axis=1)


def right_table(table):
    high, low = halves(table)
    return np.concatenate([high, high, low], axis=0)


def make_tables(parts):
    freq = np.arange(NF) - (NF - 1) // 2

    def waves(positions, rows):
        phase = 2.0 * math.pi * ((freq[:, None] * positions[None, :]) % EXT) / EXT
        pad = ((0, rows - NF), (0, 0))
        return np.pad(np.cos(phase), pad), np.pad(np.sin(phase), pad)

    core = np.arange(TILE) + HALO
    cos_full, sin_full = waves(np.arange(EXT), FP)
    cos_rows, sin_rows = waves(core, FP)
    cos_lane, sin_lane = waves(core, GP)
    width = TILE // parts
    cols = np.concatenate([cos_lane.T, -sin_lane.T], axis=1)
    col_halves = [cols[h * width : (h + 1) * width] for h in range(parts)]
    col_high = np.stack([halves(c)[0] for c in col_halves])
    col_low = np.stack([halves(c)[1] for c in col_halves])
    col_back = np.stack([right_table(c.T) for c in col_halves])
    spec = np.block([[cos_full, sin_full], [-sin_full, cos_full]])
    rows = np.block([[cos_rows.T, -sin_rows.T], [sin_rows.T, cos_rows.T]])
    field = np.block([[cos_lane, sin_lane], [-sin_lane, cos_lane]])
    return (
        col_high,
        col_low,
        col_back,
        left_table(spec),
        left_table(spec.T),
        left_table(rows),
        left_table(rows.T),
        right_table(field),
        right_table(field.T),
    )


def split(values):
    high = values.astype(BF)
    low = (values - high.astype(jnp.float32)).astype(BF)
    return high, low


def mul(a, b):
    return jnp.dot(a, b, preferred_element_type=jnp.float32)


def data_left(values, table):
    high, low = split(values)
    return mul(jnp.concatenate([high, low, high], axis=1), table)


def data_right(table, values):
    high, low = split(values)
    return mul(table, jnp.concatenate([high, low, high], axis=0))


def flip(index, bit):
    return index + bit - 2 * bit * ((index // bit) % 2)


def kernel(
    sizes,
    latent_ref,
    target_hbm,
    table_hbm,
    socs_ref,
    dose_ref,
    focus_ref,
    level_ref,
    col_high,
    col_low,
    col_back,
    spec_tab,
    spec_back,
    row_tab,
    row_back,
    field_tab,
    field_back,
    grad_out,
    loss_out,
    mask,
    raw,
    kern,
    target,
    spec,
    field,
    slope,
    dspec,
    grad,
    peer_grad,
    upper,
    lower,
    errors,
    arrived,
    local_sem,
    mask_send,
    mask_recv,
    err_send,
    err_recv,
    grad_send,
    grad_recv,
):
    parts, groups, rows, conds, kernels, pixels, all_conds, doses = sizes
    g = lax.axis_index("grp")
    j = lax.axis_index("tile")
    i = lax.axis_index("cond")
    tiles = rows // TILE
    levels = groups.bit_length() - 1
    assert groups == 1 << levels
    inverse_area = 1.0 / (EXT * EXT)

    table_copy = pltpu.make_async_copy(
        table_hbm.at[pl.ds(pl.multiple_of(j * raw.shape[0], 8), raw.shape[0])],
        raw,
        local_sem.at[0],
    )
    table_copy.start()
    target_copy = pltpu.make_async_copy(
        target_hbm.at[pl.ds(i * rows, rows)], target, local_sem.at[1]
    )
    target_copy.start()

    errors[0] = jnp.zeros(errors.shape[1:], jnp.float32)
    upper[...] = jnp.zeros_like(upper)
    lower[...] = jnp.zeros_like(lower)

    barrier = pltpu.get_barrier_semaphore()

    def greet(core, group):
        pl.semaphore_signal(barrier, inc=1, device_id=(g, core, group), device_id_type=MESH)

    @pl.when(i > 0)
    def _():
        for d in range(parts):
            greet((j + d) % parts, i - 1)

    @pl.when(i < groups - 1)
    def _():
        for d in range(parts):
            greet((j + d) % parts, i + 1)

    for level in range(1, levels):
        greet(j, flip(i, 1 << level))
    for d in range(1, parts):
        greet((j + d) % parts, i)

    sides = jnp.where(i > 0, 1, 0) + jnp.where(i < groups - 1, 1, 0)

    mask_own = jax.nn.sigmoid(latent_ref[...]).T
    mask[j, HALO : HALO + rows, :] = mask_own
    grad[...] = jnp.zeros_like(grad)

    @pl.when(i == 0)
    def _():
        for h in range(parts):
            mask[h, 0:HALO, :] = jnp.zeros((HALO, TILE // parts), jnp.float32)

    @pl.when(i == groups - 1)
    def _():
        for h in range(parts):
            mask[h, HALO + rows :, :] = jnp.zeros((HALO, TILE // parts), jnp.float32)

    table_copy.wait()
    kern[...] = jnp.zeros_like(kern)

    def pad_kernels(c, carry):
        for k in range(kernels):
            for part in range(2):
                start = (c * kernels + k) * (2 * NF) + part
                kern[c, k, part, 0:NF, 0:NF] = raw[pl.ds(start, NF, stride=2), :]
        return carry

    lax.fori_loop(0, conds, pad_kernels, 0)

    target_copy.wait()

    pl.semaphore_wait(barrier, sides * parts + (levels - 1) + (parts - 1))

    def mask_peer(d):
        block = mask.at[j, pl.ds(HALO, rows)]
        return pltpu.make_async_remote_copy(
            block, block, mask_send.at[d], mask_recv.at[d],
            device_id=(g, (j + d) % parts, i), device_id_type=MESH,
        )

    def mask_edge(up, d):
        src = mask.at[j, pl.ds(HALO, HALO)] if up else mask.at[j, pl.ds(rows, HALO)]
        dst = mask.at[j, pl.ds(HALO + rows, HALO)] if up else mask.at[j, pl.ds(0, HALO)]
        slot = parts + (0 if up else parts) + d
        return pltpu.make_async_remote_copy(
            src, dst, mask_send.at[slot], mask_recv.at[slot],
            device_id=(g, (j + d) % parts, i - 1 if up else i + 1), device_id_type=MESH,
        )

    for d in range(1, parts):
        mask_peer(d).start()

    @pl.when(i > 0)
    def _():
        for d in range(parts):
            mask_edge(True, d).start()

    @pl.when(i < groups - 1)
    def _():
        for d in range(parts):
            mask_edge(False, d).start()

    for d in range(1, parts):
        mask_peer(d).wait()

    @pl.when(i > 0)
    def _():
        for d in range(parts):
            mask_edge(True, d).wait_send()
            mask_edge(False, d).wait_recv()

    @pl.when(i < groups - 1)
    def _():
        for d in range(parts):
            mask_edge(False, d).wait_send()
            mask_edge(True, d).wait_recv()

    for t in range(tiles):
        cols = None
        for h in range(parts):
            high, low = split(mask[h, t * TILE : t * TILE + EXT, :])
            term = mul(high, col_high[h]) + mul(low, col_high[h]) + mul(high, col_low[h])
            cols = term if cols is None else cols + term
        stacked = jnp.concatenate([cols[:, :GP], cols[:, GP:]], axis=0)
        spec[t] = data_right(spec_tab[...], stacked) * inverse_area

    cond_doses = []
    for c in range(all_conds):
        value = jnp.float32(0.0)
        for n in range(doses):
            value = jnp.where(level_ref[c] == n, dose_ref[n], value)
        cond_doses.append(value)

    def forward(index, carry):
        c = index // tiles
        t = index % tiles
        dose = jnp.float32(0.0)
        for n in range(all_conds):
            dose = jnp.where(focus_ref[n] == j * conds + c, cond_doses[n], dose)
        spec_real = spec[t, 0:FP, :]
        spec_imag = spec[t, FP:, :]
        columns = []
        for k in range(kernels):
            kern_real = kern[c, k, 0]
            kern_imag = kern[c, k, 1]
            prod = jnp.concatenate(
                [
                    kern_real * spec_real - kern_imag * spec_imag,
                    kern_real * spec_imag + kern_imag * spec_real,
                ],
                axis=0,
            )
            high, low = split(prod)
            columns.append(jnp.concatenate([high, low, high], axis=0))
        half = mul(row_tab[...], jnp.concatenate(columns, axis=1))
        left = []
        for k in range(kernels):
            part = half[:, k * GP : (k + 1) * GP]
            high, low = split(jnp.concatenate([part[:TILE], part[TILE:]], axis=1))
            left.append(jnp.concatenate([high, low, high], axis=1))
        image = mul(jnp.concatenate(left, axis=0), field_tab[...])
        field[index] = image
        intensity = jnp.zeros((TILE, TILE), jnp.float32)
        for k in range(kernels):
            part = image[k * TILE : (k + 1) * TILE]
            real, imag = part[:, :TILE], part[:, TILE:]
            intensity = intensity + socs_ref[k] * (real * real + imag * imag)
        resist = jax.nn.sigmoid(STEEPNESS * (dose * intensity - THRESHOLD))
        wanted = target[pl.ds(pl.multiple_of(t * TILE, TILE), TILE), :].astype(jnp.float32)
        missed = resist - wanted
        slope[index] = (4.0 * STEEPNESS) * dose * (missed * (resist * (1.0 - resist)))
        sums = jnp.sum(missed * missed, axis=0, keepdims=True)
        errors[0, pl.ds(c, 1), :] = errors[0, pl.ds(c, 1), :] + sums
        return carry

    lax.fori_loop(0, conds * tiles, forward, 0)

    def err_copy(n):
        if n < levels:
            device, slot = (g, j, flip(i, 1 << n)), n
        else:
            device, slot = (g, (j + n - levels + 1) % parts, i), levels
        return pltpu.make_async_remote_copy(
            errors.at[slot], arrived.at[n], err_send.at[n], err_recv.at[n],
            device_id=device, device_id_type=MESH,
        )

    def backward(index, carry):
        c = index // tiles
        t = index % tiles
        gain = slope[index]
        left = []
        for k in range(kernels):
            part = field[index, k * TILE : (k + 1) * TILE, :]
            scale = socs_ref[k] * gain
            high, low = split(
                jnp.concatenate([part[:, :TILE] * scale, part[:, TILE:] * scale], axis=1)
            )
            left.append(jnp.concatenate([high, low, high], axis=1))
        half = mul(jnp.concatenate(left, axis=0), field_back[...])
        columns = []
        for k in range(kernels):
            part = half[k * TILE : (k + 1) * TILE]
            high, low = split(jnp.concatenate([part[:, :GP], part[:, GP:]], axis=0))
            columns.append(jnp.concatenate([high, low, high], axis=0))
        prod = mul(row_back[...], jnp.concatenate(columns, axis=1))
        real = jnp.zeros((FP, GP), jnp.float32)
        imag = jnp.zeros((FP, GP), jnp.float32)
        for k in range(kernels):
            prod_real = prod[:FP, k * GP : (k + 1) * GP]
            prod_imag = prod[FP:, k * GP : (k + 1) * GP]
            kern_real = kern[c, k, 0]
            kern_imag = kern[c, k, 1]
            real = real + (kern_real * prod_real + kern_imag * prod_imag)
            imag = imag + (kern_real * prod_imag - kern_imag * prod_real)
        dspec[index, 0:FP, :] = real
        dspec[index, FP:, :] = imag
        return carry

    steps = conds * tiles
    rounds = levels + 1
    for n in range(rounds):
        copies = [err_copy(n)] if n < levels else [err_copy(levels + d) for d in range(parts - 1)]
        for copy in copies:
            copy.start()
        lax.fori_loop(n * steps // rounds, (n + 1) * steps // rounds, backward, 0)
        for copy in copies:
            copy.wait()
        if n < levels:
            errors[n + 1] = errors[n] + arrived[n]

    slots = errors.shape[1]
    valid = lax.broadcasted_iota(jnp.int32, (slots, 1), 0) < conds

    def exponents(total):
        score = SHARPNESS * jnp.sum(total, axis=1, keepdims=True) / pixels
        return jnp.where(valid, jnp.exp(score), 0.0)

    mine = exponents(errors[levels])
    sums = [mine] + [exponents(arrived[levels + d]) for d in range(parts - 1)]
    denominator = functools.reduce(jnp.add, [jnp.sum(e, axis=0, keepdims=True) for e in sums])
    weights = mine / denominator
    loss_out[...] = jnp.log(denominator) / SHARPNESS

    for t in range(tiles):
        total = jnp.zeros((2 * FP, GP), jnp.float32)
        for c in range(conds):
            total = total + weights[c : c + 1, :] * dspec[c * tiles + t]
        stacked = data_right(spec_back[...], total * inverse_area)
        wide = jnp.concatenate([stacked[:EXT], stacked[EXT:]], axis=1)
        high, low = split(wide)
        left = jnp.concatenate([high, low, high], axis=1)
        for h in range(parts):
            window = (h, slice(t * TILE, t * TILE + EXT), slice(None))
            grad[window] = grad[window] + mul(left, col_back[h])

    def grad_peer(d):
        return pltpu.make_async_remote_copy(
            grad.at[(j + d) % parts, pl.ds(HALO, rows)], peer_grad.at[d - 1],
            grad_send.at[d], grad_recv.at[d],
            device_id=(g, (j + d) % parts, i), device_id_type=MESH,
        )

    def grad_edge(up, d):
        to = (j + d) % parts
        src = grad.at[to, pl.ds(0, HALO)] if up else grad.at[to, pl.ds(HALO + rows, HALO)]
        dst = lower.at[d] if up else upper.at[d]
        slot = parts + (0 if up else parts) + d
        return pltpu.make_async_remote_copy(
            src, dst, grad_send.at[slot], grad_recv.at[slot],
            device_id=(g, to, i - 1 if up else i + 1), device_id_type=MESH,
        )

    @pl.when(i > 0)
    def _():
        for d in range(parts):
            grad_edge(True, d).start()

    @pl.when(i < groups - 1)
    def _():
        for d in range(parts):
            grad_edge(False, d).start()

    for d in range(1, parts):
        grad_peer(d).start()

    own = mask[j, HALO : HALO + rows, :]
    scale = GRAD_GAIN * (own * (1.0 - own))
    total = grad[j, HALO : HALO + rows, :]

    for d in range(1, parts):
        grad_peer(d).wait()
        total = total + peer_grad[d - 1]

    @pl.when(i > 0)
    def _():
        for d in range(parts):
            grad_edge(True, d).wait_send()
            grad_edge(False, d).wait_recv()

    @pl.when(i < groups - 1)
    def _():
        for d in range(parts):
            grad_edge(False, d).wait_send()
            grad_edge(True, d).wait_recv()

    head, tail = upper[0], lower[0]
    for d in range(1, parts):
        head = head + upper[d]
        tail = tail + lower[d]
    total = jnp.concatenate(
        [total[:HALO] + head, total[HALO : rows - HALO], total[rows - HALO :] + tail], axis=0
    )
    grad_out[...] = (total * scale).T


def shards(latent, target, kernel_table, socs_weights, dose_levels, cond_focus, cond_dose):
    parts = lax.axis_size("tile")
    groups = lax.axis_size("cond")
    rows, width = latent.shape
    kernels = kernel_table.shape[1]
    all_conds = cond_focus.shape[0]
    conds = all_conds // parts
    tiles = rows // TILE
    pixels = rows * groups * TILE
    spectra = kernel_table.transpose(0, 1, 3, 2, 4).reshape(-1, NF)
    tables = [jnp.asarray(table) for table in make_tables(parts)]
    sizes = (parts, groups, rows, conds, kernels, pixels, all_conds, dose_levels.shape[0])
    slots = -(-conds // 8) * 8
    vmem = pl.BlockSpec(memory_space=pltpu.VMEM)
    smem = pl.BlockSpec(memory_space=pltpu.SMEM)
    anywhere = pl.BlockSpec(memory_space=pl.ANY)
    f32 = jnp.float32
    levels = groups.bit_length() - 1
    mask_gradient, loss = pl.pallas_call(
        functools.partial(kernel, sizes),
        out_shape=(
            jax.ShapeDtypeStruct((width, rows), f32),
            jax.ShapeDtypeStruct((1, 1), f32),
        ),
        in_specs=[vmem, anywhere, anywhere, smem, smem, smem, smem] + [vmem] * len(tables),
        out_specs=(vmem, vmem),
        scratch_shapes=[
            pltpu.VMEM((parts, rows + 2 * HALO, width), f32),
            pltpu.VMEM((conds * kernels * 2 * NF, NF), f32),
            pltpu.VMEM((conds, kernels, 2, FP, GP), f32),
            pltpu.VMEM((rows, TILE), jnp.int32),
            pltpu.VMEM((tiles, 2 * FP, GP), f32),
            pltpu.VMEM((conds * tiles, kernels * TILE, 2 * TILE), f32),
            pltpu.VMEM((conds * tiles, TILE, TILE), f32),
            pltpu.VMEM((conds * tiles, 2 * FP, GP), f32),
            pltpu.VMEM((parts, rows + 2 * HALO, width), f32),
            pltpu.VMEM((max(parts - 1, 1), rows, width), f32),
            pltpu.VMEM((parts, HALO, width), f32),
            pltpu.VMEM((parts, HALO, width), f32),
            pltpu.VMEM((levels + 1, slots, TILE), f32),
            pltpu.VMEM((levels + parts - 1, slots, TILE), f32),
            pltpu.SemaphoreType.DMA((2,)),
            pltpu.SemaphoreType.DMA((3 * parts,)),
            pltpu.SemaphoreType.DMA((3 * parts,)),
            pltpu.SemaphoreType.DMA((levels + parts - 1,)),
            pltpu.SemaphoreType.DMA((levels + parts - 1,)),
            pltpu.SemaphoreType.DMA((3 * parts,)),
            pltpu.SemaphoreType.DMA((3 * parts,)),
        ],
        compiler_params=pltpu.CompilerParams(
            collective_id=0, has_side_effects=True, vmem_limit_bytes=56 * 1024 * 1024
        ),
        name="litho",
    )(
        latent.T, target, spectra, socs_weights, dose_levels, cond_focus, cond_dose, *tables
    )
    return (mask_gradient.T, loss.reshape(1))


def solution(mesh):
    in_specs = (P(("grp", "cond"), "tile"), P("grp", None), P(), P(), P(), P(), P())
    out_specs = (P(("grp", "cond"), "tile"), P("grp"))
    return jax.shard_map(shards, mesh=mesh, in_specs=in_specs, out_specs=out_specs, check_vma=False)
```

```python
import functools
import math

import jax
import jax.numpy as jnp
import ml_dtypes
import numpy as np
from jax import lax
from jax.experimental import pallas as pl
from jax.experimental.pallas import tpu as pltpu
from jax.sharding import PartitionSpec as P

TILE = 128
HALO = 16
NF = 65
EXT = 160
FP = 80
GP = 128

STEEPNESS = 4.0
THRESHOLD = 1.0
SHARPNESS = 6.0
GRAD_GAIN = 256.0
MESH = pl.DeviceIdType.MESH
BF = jnp.bfloat16


def halves(table):
    high = table.astype(np.float32).astype(ml_dtypes.bfloat16)
    low = (table - high.astype(np.float64)).astype(np.float32).astype(ml_dtypes.bfloat16)
    return high, low


def left_table(table):
    high, low = halves(table)
    return np.concatenate([high, high, low], axis=1)


def right_table(table):
    high, low = halves(table)
    return np.concatenate([high, high, low], axis=0)


def make_tables(parts):
    freq = np.arange(NF) - (NF - 1) // 2

    def waves(positions, rows):
        phase = 2.0 * math.pi * ((freq[:, None] * positions[None, :]) % EXT) / EXT
        pad = ((0, rows - NF), (0, 0))
        return np.pad(np.cos(phase), pad), np.pad(np.sin(phase), pad)

    core = np.arange(TILE) + HALO
    cos_full, sin_full = waves(np.arange(EXT), FP)
    cos_rows, sin_rows = waves(core, FP)
    cos_lane, sin_lane = waves(core, GP)
    width = TILE // parts
    cols = np.concatenate([cos_lane.T, -sin_lane.T], axis=1)
    col_halves = [cols[h * width : (h + 1) * width] for h in range(parts)]
    col_high = np.stack([halves(c)[0] for c in col_halves])
    col_low = np.stack([halves(c)[1] for c in col_halves])
    col_back = np.stack([right_table(c.T) for c in col_halves])
    spec = np.block([[cos_full, sin_full], [-sin_full, cos_full]])
    rows = np.block([[cos_rows.T, -sin_rows.T], [sin_rows.T, cos_rows.T]])
    field = np.block([[cos_lane, sin_lane], [-sin_lane, cos_lane]])
    return (
        col_high,
        col_low,
        col_back,
        left_table(spec),
        left_table(spec.T),
        left_table(rows),
        left_table(rows.T),
        right_table(field),
        right_table(field.T),
    )


def split(values):
    high = values.astype(BF)
    low = (values - high.astype(jnp.float32)).astype(BF)
    return high, low


def mul(a, b):
    return jnp.dot(a, b, preferred_element_type=jnp.float32)


def data_left(values, table):
    high, low = split(values)
    return mul(jnp.concatenate([high, low, high], axis=1), table)


def data_right(table, values):
    high, low = split(values)
    return mul(table, jnp.concatenate([high, low, high], axis=0))


def flip(index, bit):
    return index + bit - 2 * bit * ((index // bit) % 2)


def kernel(
    sizes,
    latent_ref,
    target_hbm,
    table_hbm,
    socs_ref,
    dose_ref,
    focus_ref,
    level_ref,
    col_high_hbm,
    col_low_hbm,
    col_back_hbm,
    spec_tab_hbm,
    spec_back_hbm,
    row_tab_hbm,
    row_back_hbm,
    field_tab_hbm,
    field_back_hbm,
    grad_out,
    loss_out,
    col_high,
    col_low,
    col_back,
    spec_tab,
    spec_back,
    row_tab,
    row_back,
    field_tab,
    field_back,
    mask,
    raw,
    kern,
    target,
    spec,
    field,
    slope,
    dspec,
    grad,
    peer_grad,
    upper,
    lower,
    errors,
    arrived,
    local_sem,
    wave_sem,
    mask_send,
    mask_recv,
    err_send,
    err_recv,
    grad_send,
    grad_recv,
):
    parts, groups, rows, conds, kernels, pixels, all_conds, doses = sizes
    g = lax.axis_index("grp")
    j = lax.axis_index("tile")
    i = lax.axis_index("cond")
    tiles = rows // TILE
    levels = groups.bit_length() - 1
    assert groups == 1 << levels
    inverse_area = 1.0 / (EXT * EXT)

    table_copy = pltpu.make_async_copy(
        table_hbm.at[pl.ds(pl.multiple_of(j * raw.shape[0], 8), raw.shape[0])],
        raw,
        local_sem.at[0],
    )
    table_copy.start()
    target_copy = pltpu.make_async_copy(
        target_hbm.at[pl.ds(i * rows, rows)], target, local_sem.at[1]
    )
    target_copy.start()

    waves = (
        (col_high_hbm, col_high),
        (col_low_hbm, col_low),
        (spec_tab_hbm, spec_tab),
        (row_tab_hbm, row_tab),
        (field_tab_hbm, field_tab),
        (field_back_hbm, field_back),
        (row_back_hbm, row_back),
        (spec_back_hbm, spec_back),
        (col_back_hbm, col_back),
    )
    wave_copies = [
        pltpu.make_async_copy(src, dst, wave_sem.at[n]) for n, (src, dst) in enumerate(waves)
    ]
    for copy in wave_copies:
        copy.start()

    errors[0] = jnp.zeros(errors.shape[1:], jnp.float32)
    upper[...] = jnp.zeros_like(upper)
    lower[...] = jnp.zeros_like(lower)

    barrier = pltpu.get_barrier_semaphore()

    def greet(core, group):
        pl.semaphore_signal(barrier, inc=1, device_id=(g, core, group), device_id_type=MESH)

    @pl.when(i > 0)
    def _():
        for d in range(parts):
            greet((j + d) % parts, i - 1)

    @pl.when(i < groups - 1)
    def _():
        for d in range(parts):
            greet((j + d) % parts, i + 1)

    for level in range(1, levels):
        greet(j, flip(i, 1 << level))
    for d in range(1, parts):
        greet((j + d) % parts, i)

    sides = jnp.where(i > 0, 1, 0) + jnp.where(i < groups - 1, 1, 0)

    mask_own = jax.nn.sigmoid(latent_ref[...]).T
    mask[j, HALO : HALO + rows, :] = mask_own
    grad[...] = jnp.zeros_like(grad)

    @pl.when(i == 0)
    def _():
        for h in range(parts):
            mask[h, 0:HALO, :] = jnp.zeros((HALO, TILE // parts), jnp.float32)

    @pl.when(i == groups - 1)
    def _():
        for h in range(parts):
            mask[h, HALO + rows :, :] = jnp.zeros((HALO, TILE // parts), jnp.float32)

    table_copy.wait()
    kern[...] = jnp.zeros_like(kern)

    def pad_kernels(c, carry):
        for k in range(kernels):
            for part in range(2):
                start = (c * kernels + k) * (2 * NF) + part
                kern[c, k, part, 0:NF, 0:NF] = raw[pl.ds(start, NF, stride=2), :]
        return carry

    lax.fori_loop(0, conds, pad_kernels, 0)

    target_copy.wait()
    for copy in wave_copies:
        copy.wait()

    pl.semaphore_wait(barrier, sides * parts + (levels - 1) + (parts - 1))

    def mask_peer(d):
        block = mask.at[j, pl.ds(HALO, rows)]
        return pltpu.make_async_remote_copy(
            block, block, mask_send.at[d], mask_recv.at[d],
            device_id=(g, (j + d) % parts, i), device_id_type=MESH,
        )

    def mask_edge(up, d):
        src = mask.at[j, pl.ds(HALO, HALO)] if up else mask.at[j, pl.ds(rows, HALO)]
        dst = mask.at[j, pl.ds(HALO + rows, HALO)] if up else mask.at[j, pl.ds(0, HALO)]
        slot = parts + (0 if up else parts) + d
        return pltpu.make_async_remote_copy(
            src, dst, mask_send.at[slot], mask_recv.at[slot],
            device_id=(g, (j + d) % parts, i - 1 if up else i + 1), device_id_type=MESH,
        )

    for d in range(1, parts):
        mask_peer(d).start()

    @pl.when(i > 0)
    def _():
        for d in range(parts):
            mask_edge(True, d).start()

    @pl.when(i < groups - 1)
    def _():
        for d in range(parts):
            mask_edge(False, d).start()

    for d in range(1, parts):
        mask_peer(d).wait()

    @pl.when(i > 0)
    def _():
        for d in range(parts):
            mask_edge(True, d).wait_send()
            mask_edge(False, d).wait_recv()

    @pl.when(i < groups - 1)
    def _():
        for d in range(parts):
            mask_edge(False, d).wait_send()
            mask_edge(True, d).wait_recv()

    for t in range(tiles):
        cols = None
        for h in range(parts):
            high, low = split(mask[h, t * TILE : t * TILE + EXT, :])
            term = mul(high, col_high[h]) + mul(low, col_high[h]) + mul(high, col_low[h])
            cols = term if cols is None else cols + term
        stacked = jnp.concatenate([cols[:, :GP], cols[:, GP:]], axis=0)
        spec[t] = data_right(spec_tab[...], stacked) * inverse_area

    cond_doses = []
    for c in range(all_conds):
        value = jnp.float32(0.0)
        for n in range(doses):
            value = jnp.where(level_ref[c] == n, dose_ref[n], value)
        cond_doses.append(value)

    def forward(index, carry):
        c = index // tiles
        t = index % tiles
        dose = jnp.float32(0.0)
        for n in range(all_conds):
            dose = jnp.where(focus_ref[n] == j * conds + c, cond_doses[n], dose)
        spec_real = spec[t, 0:FP, :]
        spec_imag = spec[t, FP:, :]
        columns = []
        for k in range(kernels):
            kern_real = kern[c, k, 0]
            kern_imag = kern[c, k, 1]
            prod = jnp.concatenate(
                [
                    kern_real * spec_real - kern_imag * spec_imag,
                    kern_real * spec_imag + kern_imag * spec_real,
                ],
                axis=0,
            )
            high, low = split(prod)
            columns.append(jnp.concatenate([high, low, high], axis=0))
        half = mul(row_tab[...], jnp.concatenate(columns, axis=1))
        left = []
        for k in range(kernels):
            part = half[:, k * GP : (k + 1) * GP]
            high, low = split(jnp.concatenate([part[:TILE], part[TILE:]], axis=1))
            left.append(jnp.concatenate([high, low, high], axis=1))
        image = mul(jnp.concatenate(left, axis=0), field_tab[...])
        field[index] = image
        intensity = jnp.zeros((TILE, TILE), jnp.float32)
        for k in range(kernels):
            part = image[k * TILE : (k + 1) * TILE]
            real, imag = part[:, :TILE], part[:, TILE:]
            intensity = intensity + socs_ref[k] * (real * real + imag * imag)
        resist = jax.nn.sigmoid(STEEPNESS * (dose * intensity - THRESHOLD))
        wanted = target[pl.ds(pl.multiple_of(t * TILE, TILE), TILE), :].astype(jnp.float32)
        missed = resist - wanted
        slope[index] = (4.0 * STEEPNESS) * dose * (missed * (resist * (1.0 - resist)))
        sums = jnp.sum(missed * missed, axis=0, keepdims=True)
        errors[0, pl.ds(c, 1), :] = errors[0, pl.ds(c, 1), :] + sums
        return carry

    lax.fori_loop(0, conds * tiles, forward, 0, unroll=2)

    def err_copy(n):
        if n < levels:
            device, slot = (g, j, flip(i, 1 << n)), n
        else:
            device, slot = (g, (j + n - levels + 1) % parts, i), levels
        return pltpu.make_async_remote_copy(
            errors.at[slot], arrived.at[n], err_send.at[n], err_recv.at[n],
            device_id=device, device_id_type=MESH,
        )

    def backward(index, carry):
        c = index // tiles
        t = index % tiles
        gain = slope[index]
        left = []
        for k in range(kernels):
            part = field[index, k * TILE : (k + 1) * TILE, :]
            scale = socs_ref[k] * gain
            high, low = split(
                jnp.concatenate([part[:, :TILE] * scale, part[:, TILE:] * scale], axis=1)
            )
            left.append(jnp.concatenate([high, low, high], axis=1))
        half = mul(jnp.concatenate(left, axis=0), field_back[...])
        columns = []
        for k in range(kernels):
            part = half[k * TILE : (k + 1) * TILE]
            high, low = split(jnp.concatenate([part[:, :GP], part[:, GP:]], axis=0))
            columns.append(jnp.concatenate([high, low, high], axis=0))
        prod = mul(row_back[...], jnp.concatenate(columns, axis=1))
        real = jnp.zeros((FP, GP), jnp.float32)
        imag = jnp.zeros((FP, GP), jnp.float32)
        for k in range(kernels):
            prod_real = prod[:FP, k * GP : (k + 1) * GP]
            prod_imag = prod[FP:, k * GP : (k + 1) * GP]
            kern_real = kern[c, k, 0]
            kern_imag = kern[c, k, 1]
            real = real + (kern_real * prod_real + kern_imag * prod_imag)
            imag = imag + (kern_real * prod_imag - kern_imag * prod_real)
        dspec[index, 0:FP, :] = real
        dspec[index, FP:, :] = imag
        return carry

    steps = conds * tiles
    rounds = levels + 1
    for n in range(rounds):
        copies = [err_copy(n)] if n < levels else [err_copy(levels + d) for d in range(parts - 1)]
        for copy in copies:
            copy.start()
        lax.fori_loop(n * steps // rounds, (n + 1) * steps // rounds, backward, 0, unroll=2)
        for copy in copies:
            copy.wait()
        if n < levels:
            errors[n + 1] = errors[n] + arrived[n]

    slots = errors.shape[1]
    valid = lax.broadcasted_iota(jnp.int32, (slots, 1), 0) < conds

    def exponents(total):
        score = SHARPNESS * jnp.sum(total, axis=1, keepdims=True) / pixels
        return jnp.where(valid, jnp.exp(score), 0.0)

    mine = exponents(errors[levels])
    sums = [mine] + [exponents(arrived[levels + d]) for d in range(parts - 1)]
    denominator = functools.reduce(jnp.add, [jnp.sum(e, axis=0, keepdims=True) for e in sums])
    weights = mine / denominator
    loss_out[...] = jnp.log(denominator) / SHARPNESS

    for t in range(tiles):
        total = jnp.zeros((2 * FP, GP), jnp.float32)
        for c in range(conds):
            total = total + weights[c : c + 1, :] * dspec[c * tiles + t]
        stacked = data_right(spec_back[...], total * inverse_area)
        wide = jnp.concatenate([stacked[:EXT], stacked[EXT:]], axis=1)
        high, low = split(wide)
        left = jnp.concatenate([high, low, high], axis=1)
        for h in range(parts):
            window = (h, slice(t * TILE, t * TILE + EXT), slice(None))
            grad[window] = grad[window] + mul(left, col_back[h])

    def grad_peer(d):
        return pltpu.make_async_remote_copy(
            grad.at[(j + d) % parts, pl.ds(HALO, rows)], peer_grad.at[d - 1],
            grad_send.at[d], grad_recv.at[d],
            device_id=(g, (j + d) % parts, i), device_id_type=MESH,
        )

    def grad_edge(up, d):
        to = (j + d) % parts
        src = grad.at[to, pl.ds(0, HALO)] if up else grad.at[to, pl.ds(HALO + rows, HALO)]
        dst = lower.at[d] if up else upper.at[d]
        slot = parts + (0 if up else parts) + d
        return pltpu.make_async_remote_copy(
            src, dst, grad_send.at[slot], grad_recv.at[slot],
            device_id=(g, to, i - 1 if up else i + 1), device_id_type=MESH,
        )

    @pl.when(i > 0)
    def _():
        for d in range(parts):
            grad_edge(True, d).start()

    @pl.when(i < groups - 1)
    def _():
        for d in range(parts):
            grad_edge(False, d).start()

    for d in range(1, parts):
        grad_peer(d).start()

    own = mask[j, HALO : HALO + rows, :]
    scale = GRAD_GAIN * (own * (1.0 - own))
    total = grad[j, HALO : HALO + rows, :]

    for d in range(1, parts):
        grad_peer(d).wait()
        total = total + peer_grad[d - 1]

    @pl.when(i > 0)
    def _():
        for d in range(parts):
            grad_edge(True, d).wait_send()
            grad_edge(False, d).wait_recv()

    @pl.when(i < groups - 1)
    def _():
        for d in range(parts):
            grad_edge(False, d).wait_send()
            grad_edge(True, d).wait_recv()

    head, tail = upper[0], lower[0]
    for d in range(1, parts):
        head = head + upper[d]
        tail = tail + lower[d]
    total = jnp.concatenate(
        [total[:HALO] + head, total[HALO : rows - HALO], total[rows - HALO :] + tail], axis=0
    )
    grad_out[...] = (total * scale).T


def shards(latent, target, kernel_table, socs_weights, dose_levels, cond_focus, cond_dose):
    parts = lax.axis_size("tile")
    groups = lax.axis_size("cond")
    rows, width = latent.shape
    kernels = kernel_table.shape[1]
    all_conds = cond_focus.shape[0]
    conds = all_conds // parts
    tiles = rows // TILE
    pixels = rows * groups * TILE
    spectra = kernel_table.transpose(0, 1, 3, 2, 4).reshape(-1, NF)
    tables = [jnp.asarray(table) for table in make_tables(parts)]
    sizes = (parts, groups, rows, conds, kernels, pixels, all_conds, dose_levels.shape[0])
    slots = -(-conds // 8) * 8
    vmem = pl.BlockSpec(memory_space=pltpu.VMEM)
    smem = pl.BlockSpec(memory_space=pltpu.SMEM)
    anywhere = pl.BlockSpec(memory_space=pl.ANY)
    f32 = jnp.float32
    levels = groups.bit_length() - 1
    mask_gradient, loss = pl.pallas_call(
        functools.partial(kernel, sizes),
        out_shape=(
            jax.ShapeDtypeStruct((width, rows), f32),
            jax.ShapeDtypeStruct((1, 1), f32),
        ),
        in_specs=[vmem, anywhere, anywhere, smem, smem, smem, smem] + [anywhere] * len(tables),
        out_specs=(vmem, vmem),
        scratch_shapes=[pltpu.VMEM(table.shape, table.dtype) for table in tables]
        + [
            pltpu.VMEM((parts, rows + 2 * HALO, width), f32),
            pltpu.VMEM((conds * kernels * 2 * NF, NF), f32),
            pltpu.VMEM((conds, kernels, 2, FP, GP), f32),
            pltpu.VMEM((rows, TILE), jnp.int32),
            pltpu.VMEM((tiles, 2 * FP, GP), f32),
            pltpu.VMEM((conds * tiles, kernels * TILE, 2 * TILE), f32),
            pltpu.VMEM((conds * tiles, TILE, TILE), f32),
            pltpu.VMEM((conds * tiles, 2 * FP, GP), f32),
            pltpu.VMEM((parts, rows + 2 * HALO, width), f32),
            pltpu.VMEM((max(parts - 1, 1), rows, width), f32),
            pltpu.VMEM((parts, HALO, width), f32),
            pltpu.VMEM((parts, HALO, width), f32),
            pltpu.VMEM((levels + 1, slots, TILE), f32),
            pltpu.VMEM((levels + parts - 1, slots, TILE), f32),
            pltpu.SemaphoreType.DMA((2,)),
            pltpu.SemaphoreType.DMA((len(tables),)),
            pltpu.SemaphoreType.DMA((3 * parts,)),
            pltpu.SemaphoreType.DMA((3 * parts,)),
            pltpu.SemaphoreType.DMA((levels + parts - 1,)),
            pltpu.SemaphoreType.DMA((levels + parts - 1,)),
            pltpu.SemaphoreType.DMA((3 * parts,)),
            pltpu.SemaphoreType.DMA((3 * parts,)),
        ],
        compiler_params=pltpu.CompilerParams(
            collective_id=0, has_side_effects=True, vmem_limit_bytes=56 * 1024 * 1024
        ),
        name="litho",
    )(
        latent.T, target, spectra, socs_weights, dose_levels, cond_focus, cond_dose, *tables
    )
    return (mask_gradient.T, loss.reshape(1))


def solution(mesh):
    in_specs = (P(("grp", "cond"), "tile"), P("grp", None), P(), P(), P(), P(), P())
    out_specs = (P(("grp", "cond"), "tile"), P("grp"))
    return jax.shard_map(shards, mesh=mesh, in_specs=in_specs, out_specs=out_specs, check_vma=False)
```
